128 devices in a mesh: side: 2 (over core), dev: 64 (over y, z, x).
Axes of the slice: x: 4, y: 4, z: 4, core: 2. Of those that a mesh axis runs over, the one named last changes fastest.
Arguments:
- query: bfloat16 [1024, 8, 128], P('dev', 'side'), may hold values from -6 to 6
- key_in: bfloat16 [1024, 8, 128], P('dev', 'side'), may hold values from -6 to 6
- value: bfloat16 [1024, 16, 128], P('dev', 'side'), may hold values from -6 to 6
- out_gate: bfloat16 [1024, 16, 128], P('dev', 'side'), may hold values from -6 to 6
- decay_arg: float32 [1024, 16], P('dev', 'side'), may hold values from -6 to 6
- beta_arg: float32 [1024, 16], P('dev', 'side'), may hold values from -8 to 8
- decay_log: float32 [16], P('side'), may hold values from -3 to 1
- step_bias: float32 [16], P('side'), may hold values from -2 to 1
- states: float32 [1024, 16, 128, 128], P('dev', 'side'), may hold values from -6 to 6
- norm_gain: float32 [128], replicated, may hold values from 0.25 to 1.75
- out_weight: bfloat16 [2048, 2048], P('side'), may hold values from -0.125 to 0.125
- residual: bfloat16 [1024, 2048], P('dev'), may hold values from -3 to 3
- post_gain: float32 [2048], replicated, may hold values from 0.25 to 1.75
- route_ids: int32 [1024, 10], P('dev'), may hold values from 0 to 255, all different within a row; in each aligned block of 16 rows (0 to 15, 16 to 31, ...) at most 3 rows name the same one
- route_weight: float32 [1024, 10], P('dev'), may hold values from 0.05 to 0.5
- w_gate: bfloat16 [256, 2048, 512], P(('side', 'dev')), may hold values from -0.125 to 0.125
- w_up: bfloat16 [256, 2048, 512], P(('side', 'dev')), may hold values from -0.125 to 0.125
- w_down: bfloat16 [256, 512, 2048], P(('side', 'dev')), may hold values from -0.25 to 0.25
Outputs:
- mixed: bfloat16 [1024, 2048], P('dev', 'side')
The draws below stay inside these ranges and needn't reach their ends.
Inputs may be any that keep to these rules, and one draw needn't show every extreme that they name: `route_ids`: A token's 10 experts are distinct; among the 16 tokens of one index of dev, no expert is named more than 3 times.
All inputs are finite; a program needn't handle non-finite values.
Results may differ from the reference program's by a relative error of at most 0.0059.
Values may be sent and summed in bfloat16 or wider, within the bound.
No kernel may reach another device: no remote copies, remote signals or barrier semaphores. Data moves between devices by JAX's collectives and lax.ppermute only.
A program may use at most 128 MiB of HBM per device.

```python
import math
import jax
import jax.numpy as jnp
import numpy as np
from jax import lax

D = 2048
HV = 16
HK = 8
DK = 128
DV = 128
FFE = 512
TOP = 10
CAP = 3
TOK_DEV = 16
TOKENS = 1024
EXPERTS = 256
N_DEV = 64


def block_levels(rng, extent, cuts, low, largest):
    factor_of = 1.0
    for axis_at, blocks in cuts:
        draws = jax.random.uniform(jax.random.fold_in(jax.random.fold_in(rng, 6), axis_at), (blocks,), jnp.float32, low / len(cuts), largest / len(cuts))
        factor_of = factor_of * jnp.repeat(jnp.exp(draws), extent[axis_at] // blocks).reshape((-1,) + (1,) * (len(extent) - 1 - axis_at))
    return factor_of


def deal_out(rng, own, number, rows, number_of, top, bound, skew):
    ranking = jax.random.permutation(rng, number_of)
    crowded, common = shares(number_of, rows * top, bound, skew, True), shares(number_of, rows * top, bound, skew, False)
    places = jnp.arange(number_of)

    def named(tallies, rotation):
        used = int((tallies > 0).sum())
        fixed = max(1, used // 4)
        passed = fixed + (places - fixed + rotation * (used - fixed)) % max(1, number_of - fixed)
        return jnp.zeros((number_of,), jnp.int32).at[ranking[jnp.where(places < fixed, places, passed)]].set(jnp.asarray(tallies, jnp.int32))

    tallies = jnp.where(number % 4 == 0, named(crowded, number // 4), named(common, number - number // 4 - 1))
    mixed = jax.random.permutation(jax.random.fold_in(own, 3), number_of)
    giver, sink = mixed[0:number_of // 2 * 2:2], mixed[1:number_of // 2 * 2:2]
    slack = jnp.minimum(tallies[giver] - 1, bound - tallies[sink]) // 2
    slack = jnp.where((giver == ranking[0]) | (sink == ranking[0]) | (tallies[sink] == 0), 0, jnp.maximum(slack, 0))
    passed = jax.random.randint(jax.random.fold_in(own, 4), (number_of // 2,), 0, 1 << 20) % (slack + 1)
    tallies = tallies.at[giver].add(-passed).at[sink].add(passed)
    items = jnp.searchsorted(jnp.cumsum(tallies), jnp.arange(rows * top), side="right").astype(jnp.int32)
    grid = items.reshape(top, rows).T
    grid = grid[jax.random.permutation(jax.random.fold_in(own, 1), rows)]
    rotation = jax.random.randint(jax.random.fold_in(own, 2), (rows, 1), 0, top)
    return jnp.take_along_axis(grid, (jnp.arange(top)[None, :] + rotation) % top, axis=1)


def shares(count, total, most, skew, full):
    weights = [(1 << 20) // math.isqrt(standing ** skew) + 1 for standing in range(1, count + 1)]
    largest = most if full else min(most, max(-(-total // count), total * weights[0] // sum(weights)))
    least = 1 if total - largest >= count - 1 else 0
    given, surplus = [largest] + [least] * (count - 1), total - largest - least * (count - 1)
    while surplus > 0:
        candidates = [i for i in range(1, count) if given[i] < largest] or [i for i in range(1, count) if given[i] < most]
        mass, budget = sum([weights[i] for i in candidates]), surplus
        for i in candidates:
            extra = min(most - given[i], max(1, budget * weights[i] // mass), surplus)
            given[i] = given[i] + extra
            surplus = surplus - extra
    return np.array(given)


def gaussian(stream_key, shape, scale, reach, cuts=(), kind=jnp.bfloat16):
    gain = block_levels(stream_key, shape, cuts, -0.22, 0.18) if cuts else 1.0
    drawn = jax.random.normal(stream_key, shape, jnp.float32) * scale * gain
    return jnp.minimum(jnp.maximum(drawn, -reach), reach).astype(kind)


def setup_inputs(seed: int = 0) -> dict:
    arg_keys = jax.random.split(jax.random.key(seed), 19)
    query = gaussian(arg_keys[0], (TOKENS, HK, DK), 1.0, 6.0, ((0, 64), (1, 2)))
    key_in = gaussian(arg_keys[1], (TOKENS, HK, DK), 1.0, 6.0, ((0, 64), (1, 2)))
    value = gaussian(arg_keys[2], (TOKENS, HV, DV), 1.0, 6.0, ((0, 64), (1, 2)))
    out_gate = gaussian(arg_keys[3], (TOKENS, HV, DV), 1.0, 6.0, ((0, 64), (1, 2)))
    decay_arg = gaussian(arg_keys[4], (TOKENS, HV), 1.0, 6.0, ((0, 64), (1, 2)), jnp.float32)
    beta_arg = gaussian(arg_keys[5], (TOKENS, HV), 1.5, 8.0, ((0, 64), (1, 2)), jnp.float32)
    decay_log = jnp.clip(-3.0 + 4.0 * jax.random.uniform(arg_keys[6], (HV,), jnp.float32) ** block_levels(arg_keys[6], (HV,), ((0, 2),), -0.2, 0.2), -3.0, 1.0)
    step_bias = jnp.clip(-2.0 + 3.0 * jax.random.uniform(arg_keys[7], (HV,), jnp.float32) ** block_levels(arg_keys[7], (HV,), ((0, 2),), -0.2, 0.2), -2.0, 1.0)
    states = gaussian(arg_keys[8], (TOKENS, HV, DK, DV), 1.0, 6.0, ((0, 64), (1, 2)), jnp.float32)
    norm_gain = jnp.clip(1.0 + 0.15 * jax.random.normal(arg_keys[9], (DV,), jnp.float32), 0.25, 1.75)
    out_weight = gaussian(arg_keys[10], (HV * DV, D), (HV * DV) ** -0.5, 0.125, ((0, 2),))
    residual = gaussian(arg_keys[11], (TOKENS, D), 0.5, 3.0, ((0, 64),))
    post_gain = jnp.clip(1.0 + 0.15 * jax.random.normal(arg_keys[12], (D,), jnp.float32), 0.25, 1.75)
    route_ids_keys = jax.random.split(jax.random.fold_in(arg_keys[13], 1), TOKENS // TOK_DEV)
    route_ids_turns = jax.random.permutation(jax.random.fold_in(arg_keys[13], 3), TOKENS // TOK_DEV)
    route_ids = jax.vmap(lambda own, number: deal_out(jax.random.fold_in(arg_keys[13], 2), own, number, TOK_DEV, EXPERTS, TOP, CAP, 2))(route_ids_keys, route_ids_turns).reshape((TOKENS, TOP))
    route_weight = jnp.clip(jnp.exp(math.log(0.5) - 2.3025851 * jax.random.uniform(arg_keys[14], (TOKENS, TOP), jnp.float32) ** block_levels(arg_keys[14], (TOKENS, TOP), ((0, 64),), -0.2, 0.2)), 0.05, 0.5)
    w_gate = gaussian(arg_keys[15], (EXPERTS, D, FFE), D ** -0.5, 0.125, ((0, 128),))
    w_up = gaussian(arg_keys[16], (EXPERTS, D, FFE), D ** -0.5, 0.125, ((0, 128),))
    w_down = gaussian(arg_keys[17], (EXPERTS, FFE, D), FFE ** -0.5, 0.25, ((0, 128),))
    return dict(query=query, key_in=key_in, value=value, out_gate=out_gate, decay_arg=decay_arg, beta_arg=beta_arg, decay_log=decay_log, step_bias=step_bias, states=states, norm_gain=norm_gain, out_weight=out_weight, residual=residual, post_gain=post_gain, route_ids=route_ids, route_weight=route_weight, w_gate=w_gate, w_up=w_up, w_down=w_down)


EPSILON = 1e-06
TOP_PREC = lax.Precision.HIGHEST

def unit_rows(source):
    source = source.astype(jnp.float32)
    return source * lax.rsqrt(lax.optimization_barrier(jnp.sum(source * source, -1, keepdims=True)) + EPSILON)

def delta_heads(query, key_in, value, out_gate, decay_arg, beta_arg, decay_log, step_bias, states, norm_gain):
    repeats = value.shape[1] // query.shape[1]
    query_unit = jnp.repeat(unit_rows(query), repeats, axis=1) * query.shape[2] ** (-0.5)
    key_unit = jnp.repeat(unit_rows(key_in), repeats, axis=1)
    retain = jnp.exp(-jnp.exp(decay_log) * jax.nn.softplus(decay_arg + step_bias))
    write_rate = jax.nn.sigmoid(beta_arg)
    kstate = jnp.einsum('thi,thij->thj', key_unit, states, precision=TOP_PREC)
    qstate = jnp.einsum('thi,thij->thj', query_unit, states, precision=TOP_PREC)
    correct = write_rate[..., None] * (value.astype(jnp.float32) - retain[..., None] * kstate)
    attend = retain[..., None] * qstate + lax.optimization_barrier(jnp.sum(query_unit * key_unit, -1, keepdims=True)) * correct
    inv_rms = lax.rsqrt(lax.optimization_barrier(jnp.mean(attend * attend, -1, keepdims=True)) + EPSILON)
    gated_out = attend * inv_rms * norm_gain * jax.nn.silu(out_gate.astype(jnp.float32))
    return gated_out.astype(jnp.bfloat16).reshape(value.shape[0], value.shape[1] * value.shape[2])

def reference(query, key_in, value, out_gate, decay_arg, beta_arg, decay_log, step_bias, states, norm_gain, out_weight, residual, post_gain, route_ids, route_weight, w_gate, w_up, w_down):
    gated_out = delta_heads(query, key_in, value, out_gate, decay_arg, beta_arg, decay_log, step_bias, states, norm_gain)
    hidden = residual.astype(jnp.float32) + jnp.dot(gated_out, out_weight, preferred_element_type=jnp.float32)
    inv_rms = lax.rsqrt(lax.optimization_barrier(jnp.mean(hidden * hidden, -1, keepdims=True)) + EPSILON)
    moe_input = (hidden * inv_rms * post_gain).astype(jnp.bfloat16)
    flat_ids = route_ids.reshape(-1)
    flat_weight = route_weight.reshape(-1)
    rows_most = N_DEV * CAP

    def one_expert(expert_sum, expert):
        slot_hit = flat_ids == expert
        entries = jnp.sum(slot_hit.astype(jnp.int32))
        picked = jnp.nonzero(slot_hit, size=rows_most, fill_value=0)[0].astype(jnp.int32)
        weights = jnp.where(jnp.arange(rows_most, dtype=jnp.int32) < entries, flat_weight[picked], jnp.float32(0.0))
        token_index = (picked // TOP).astype(jnp.int32)
        chosen = moe_input[token_index]
        gate_act = jnp.dot(chosen, w_gate[expert], preferred_element_type=jnp.float32)
        up_act = jnp.dot(chosen, w_up[expert], preferred_element_type=jnp.float32)
        inner = (jax.nn.silu(gate_act) * up_act).astype(jnp.bfloat16)
        expert_out = jnp.dot(inner, w_down[expert], preferred_element_type=jnp.float32).astype(jnp.bfloat16)
        expert_sum = expert_sum.at[token_index].add(weights[:, None] * expert_out.astype(jnp.float32))
        return (expert_sum, None)
    expert_sum, unused = lax.scan(one_expert, jnp.zeros(hidden.shape, jnp.float32), jnp.arange(EXPERTS, dtype=jnp.int32))
    return (hidden + expert_sum).astype(jnp.bfloat16)
```

```python
import jax
import jax.numpy as jnp
from jax import lax
from jax.experimental import pallas as pl
from jax.experimental.pallas import tpu as pltpu
from jax.sharding import PartitionSpec as P

CAP = 3
EPSILON = 1e-06
LANES = 128
TILE = 16
STEP_TOKENS = 2
MIB = 1 << 20


def softplus(x):
    return jnp.maximum(x, 0.0) + jnp.log1p(jnp.exp(-jnp.abs(x)))


def sigmoid(x):
    return 1.0 / (1.0 + jnp.exp(-x))


def unit_rows(source):
    return source * lax.rsqrt(jnp.sum(source * source, -1, keepdims=True) + EPSILON)


def row_to_column(row):
    n = row.shape[1]
    square = jnp.broadcast_to(row, (n, n))
    on_diagonal = lax.broadcasted_iota(jnp.int32, (n, n), 0) == lax.broadcasted_iota(
        jnp.int32, (n, n), 1
    )
    return jnp.sum(jnp.where(on_diagonal, square, 0.0), axis=1, keepdims=True)


def pick_column(table, column):
    lane = lax.broadcasted_iota(jnp.int32, table.shape, 1)
    return jnp.sum(jnp.where(lane == column, table, 0.0), axis=1, keepdims=True)


def delta_kernel(
    side_ref,
    query_ref,
    key_ref,
    value_ref,
    gate_ref,
    decay_ref,
    beta_ref,
    log_ref,
    bias_ref,
    state_ref,
    gain_ref,
    residual_ref,
    weight_hbm,
    out_ref,
    weight_ref,
    heads_ref,
    weight_sem,
):
    step = pl.program_id(0)
    steps = pl.num_programs(0)
    tokens, width = residual_ref.shape
    heads = value_ref.shape[1]
    key_heads = query_ref.shape[1]
    repeats = heads // key_heads
    size = query_ref.shape[2]
    load = pltpu.make_async_copy(weight_hbm, weight_ref, weight_sem)

    @pl.when(step == 0)
    def _():
        load.start()

    retain_all = jnp.exp(
        -jnp.exp(row_to_column(log_ref[...]))
        * softplus(decay_ref[...] + row_to_column(bias_ref[...]))
    )
    rate_all = sigmoid(beta_ref[...])
    units = []
    for j in range(STEP_TOKENS):
        units.append(unit_rows(query_ref[j].astype(jnp.float32)) * size ** (-0.5))
        units.append(unit_rows(key_ref[j].astype(jnp.float32)))
    rows = jnp.concatenate(units, 0)
    columns = rows.T
    for j in range(STEP_TOKENS):
        token = step * STEP_TOKENS + j
        query_unit, key_unit = units[2 * j], units[2 * j + 1]
        products = jnp.sum(query_unit * key_unit, -1, keepdims=True)
        qrows, krows, prows = [], [], []
        for k in range(key_heads):
            at = 2 * j * key_heads + k
            qcol = jnp.broadcast_to(columns[:, at : at + 1], (size, size))
            at = at + key_heads
            kcol = jnp.broadcast_to(columns[:, at : at + 1], (size, size))
            for r in range(repeats):
                state = state_ref[j, k * repeats + r]
                qrows.append(jnp.sum(qcol * state, axis=0, keepdims=True))
                krows.append(jnp.sum(kcol * state, axis=0, keepdims=True))
                prows.append(products[k : k + 1])
        qstate = jnp.concatenate(qrows, 0)
        kstate = jnp.concatenate(krows, 0)
        product = jnp.concatenate(prows, 0)
        retain = pick_column(retain_all, token)
        rate = pick_column(rate_all, token)
        correct = rate * (value_ref[j].astype(jnp.float32) - retain * kstate)
        attend = retain * qstate + product * correct
        inv_rms = lax.rsqrt(jnp.mean(attend * attend, -1, keepdims=True) + EPSILON)
        gate = gate_ref[j].astype(jnp.float32)
        gated = attend * inv_rms * gain_ref[...] * (gate * sigmoid(gate))
        heads_ref[pl.ds(pl.multiple_of(token * heads, heads), heads), :] = gated

    @pl.when(step == steps - 1)
    def _():
        gated_out = jnp.concatenate(
            [heads_ref[pl.ds(h, tokens, stride=heads), :] for h in range(heads)], 1
        ).astype(jnp.bfloat16)
        load.wait()
        side = side_ref[0]
        blocks = width // LANES
        wide = 4 * LANES
        for n in range(width // wide):
            part = jnp.dot(
                gated_out,
                weight_ref[:, n * wide : (n + 1) * wide],
                preferred_element_type=jnp.float32,
            )
            kept = residual_ref[:, n * wide : (n + 1) * wide].astype(jnp.float32)
            part = part + jnp.where(side == 0, kept, 0.0)
            for f in range(4):
                out_ref[pl.ds(n * 4 + f, tokens, stride=blocks), :] = part[
                    :, f * LANES : (f + 1) * LANES
                ]


def delta_call(side, query, key_in, value, gate, decay, beta, log, bias, states, gain, residual, weight):
    tokens, heads, size = value.shape
    key_heads = query.shape[1]
    width = residual.shape[1]

    def by_token(*shape):
        return pl.BlockSpec((STEP_TOKENS,) + shape, lambda i: (i,) + (0,) * len(shape))

    def whole(array):
        return pl.BlockSpec(array.shape, lambda i: (0,) * array.ndim)

    return pl.pallas_call(
        delta_kernel,
        grid=(tokens // STEP_TOKENS,),
        out_shape=jax.ShapeDtypeStruct((tokens * width // LANES, LANES), jnp.float32),
        in_specs=[
            pl.BlockSpec(memory_space=pltpu.SMEM),
            by_token(key_heads, size),
            by_token(key_heads, size),
            by_token(heads, size),
            by_token(heads, size),
            whole(decay),
            whole(beta),
            whole(log),
            whole(bias),
            by_token(heads, size, size),
            whole(gain),
            whole(residual),
            pl.BlockSpec(memory_space=pl.ANY),
        ],
        out_specs=pl.BlockSpec((tokens * width // LANES, LANES), lambda i: (0, 0)),
        scratch_shapes=[
            pltpu.VMEM(weight.shape, weight.dtype),
            pltpu.VMEM((tokens * heads, size), jnp.float32),
            pltpu.SemaphoreType.DMA,
        ],
        compiler_params=pltpu.CompilerParams(vmem_limit_bytes=16 * MIB),
        name="delta",
    )(side, query, key_in, value, gate, decay, beta, log, bias, states, gain, residual, weight)


def pack_kernel(source_ref, own_ref, other_ref, gain_ref, out_ref, tiles_ref):
    blocks = gain_ref.shape[0]
    tokens = own_ref.shape[0] // blocks
    for t in range(tokens):
        rows = slice(t * blocks, (t + 1) * blocks)
        hidden = own_ref[rows, :] + other_ref[rows, :]
        mean = jnp.sum(
            jnp.sum(hidden * hidden, axis=0, keepdims=True), axis=1, keepdims=True
        ) * (1.0 / (blocks * LANES))
        tiles_ref[rows, :] = (hidden * lax.rsqrt(mean + EPSILON) * gain_ref[...]).astype(
            jnp.bfloat16
        )
    tiles_ref[tokens * blocks :, :] = jnp.zeros((blocks, LANES), jnp.bfloat16)
    slots = out_ref.shape[0] // blocks
    for s in range(slots):
        at = pl.multiple_of(source_ref[s] * blocks, blocks)
        out_ref[s * blocks : (s + 1) * blocks, :] = tiles_ref[pl.ds(at, blocks), :]


def pack_call(source, own, other, gain):
    blocks = gain.shape[0]
    slots = source.shape[0]
    vmem = pl.BlockSpec(memory_space=pltpu.VMEM)
    return pl.pallas_call(
        pack_kernel,
        out_shape=jax.ShapeDtypeStruct((slots * blocks, LANES), jnp.bfloat16),
        in_specs=[pl.BlockSpec(memory_space=pltpu.SMEM), vmem, vmem, vmem],
        out_specs=vmem,
        scratch_shapes=[pltpu.VMEM((own.shape[0] + blocks, LANES), jnp.bfloat16)],
        compiler_params=pltpu.CompilerParams(vmem_limit_bytes=16 * MIB),
        name="pack",
    )(source, own, other, gain)


def expert_kernel(
    x_ref, gate_hbm, up_hbm, down_hbm, out_ref, gate_ref, up_ref, down_ref, rows_ref, sems
):
    experts, width, units = gate_hbm.shape
    sources = x_ref.shape[0]
    blocks = width // LANES
    groups = sources // TILE
    copies = []
    for e in range(experts):
        for i, (hbm, ref) in enumerate(
            ((gate_hbm, gate_ref), (up_hbm, up_ref), (down_hbm, down_ref))
        ):
            copies.append(pltpu.make_async_copy(hbm.at[e], ref.at[e], sems.at[e, i]))
            copies[-1].start()
    row = lax.broadcasted_iota(jnp.int32, (TILE * blocks, TILE * blocks), 0)
    column = lax.broadcasted_iota(jnp.int32, (TILE * blocks, TILE * blocks), 1)
    swap = jnp.where((row % TILE) * TILE + row // TILE == column, 1.0, 0.0).astype(jnp.bfloat16)
    for e in range(experts):
        for g in range(groups):
            for c in range(CAP):
                at = (e * CAP + c) * blocks
                block = x_ref[g * TILE : (g + 1) * TILE, at : at + blocks, :]
                block = block.reshape(TILE * blocks, LANES)
                turned = jnp.dot(swap, block, preferred_element_type=jnp.float32)
                turned = turned.astype(jnp.bfloat16)
                r = ((e * groups + g) * CAP + c) * TILE
                for f in range(blocks):
                    rows_ref[r : r + TILE, f * LANES : (f + 1) * LANES] = turned[
                        f * TILE : (f + 1) * TILE
                    ]
    count = groups * CAP * TILE
    for e in range(experts):
        x = rows_ref[e * count : (e + 1) * count, :]
        copies[3 * e].wait()
        gate = jnp.dot(x, gate_ref[e], preferred_element_type=jnp.float32)
        copies[3 * e + 1].wait()
        up = jnp.dot(x, up_ref[e], preferred_element_type=jnp.float32)
        inner = (gate * sigmoid(gate) * up).astype(jnp.bfloat16)
        copies[3 * e + 2].wait()
        wide = 4 * LANES
        for n in range(width // wide):
            y = jnp.dot(
                inner, down_ref[e, :, n * wide : (n + 1) * wide], preferred_element_type=jnp.float32
            )
            rows_ref[e * count : (e + 1) * count, n * wide : (n + 1) * wide] = y.astype(
                jnp.bfloat16
            )
        for g in range(groups):
            for c in range(CAP):
                r = ((e * groups + g) * CAP + c) * TILE
                block = jnp.concatenate(
                    [
                        rows_ref[r : r + TILE, f * LANES : (f + 1) * LANES]
                        for f in range(blocks)
                    ],
                    0,
                )
                turned = jnp.dot(swap, block, preferred_element_type=jnp.float32)
                at = (e * CAP + c) * blocks
                out_ref[g * TILE : (g + 1) * TILE, at : at + blocks, :] = turned.astype(
                    jnp.bfloat16
                ).reshape(TILE, blocks, LANES)


def expert_call(received, w_gate, w_up, w_down):
    experts, width, units = w_gate.shape
    vmem = pl.BlockSpec(memory_space=pltpu.VMEM)
    hbm = pl.BlockSpec(memory_space=pl.ANY)
    slots = received.shape[0] * CAP * experts
    return pl.pallas_call(
        expert_kernel,
        out_shape=jax.ShapeDtypeStruct(received.shape, received.dtype),
        in_specs=[vmem, hbm, hbm, hbm],
        out_specs=vmem,
        scratch_shapes=[
            pltpu.VMEM(w_gate.shape, w_gate.dtype),
            pltpu.VMEM(w_up.shape, w_up.dtype),
            pltpu.VMEM(w_down.shape, w_down.dtype),
            pltpu.VMEM((slots, width), jnp.bfloat16),
            pltpu.SemaphoreType.DMA((experts, 3)),
        ],
        compiler_params=pltpu.CompilerParams(vmem_limit_bytes=32 * MIB),
        name="experts",
    )(received, w_gate, w_up, w_down)


def gather_kernel(side_ref, slot_ref, weight_ref, back_ref, keep_ref, send_ref, sums_ref):
    blocks = sums_ref.shape[0]
    half = blocks // 2
    tokens = keep_ref.shape[0] // half
    top = slot_ref.shape[0] // tokens
    side = side_ref[0]
    for t in range(tokens):
        total = jnp.zeros((blocks, LANES), jnp.float32)
        for k in range(top):
            at = pl.multiple_of(slot_ref[t * top + k] * blocks, blocks)
            tile = back_ref[pl.ds(at, blocks), :].astype(jnp.float32)
            total = total + weight_ref[t * top + k] * tile
        sums_ref[...] = total
        own = pl.multiple_of(side * half, half)
        other = pl.multiple_of((1 - side) * half, half)
        keep_ref[t * half : (t + 1) * half, :] = sums_ref[pl.ds(own, half), :]
        send_ref[t * half : (t + 1) * half, :] = sums_ref[pl.ds(other, half), :]


def gather_call(side, slots, weights, back, tokens, blocks):
    vmem = pl.BlockSpec(memory_space=pltpu.VMEM)
    smem = pl.BlockSpec(memory_space=pltpu.SMEM)
    half = jax.ShapeDtypeStruct((tokens * blocks // 2, LANES), jnp.float32)
    return pl.pallas_call(
        gather_kernel,
        out_shape=(half, half),
        in_specs=[smem, smem, smem, vmem],
        out_specs=(vmem, vmem),
        scratch_shapes=[pltpu.VMEM((blocks, LANES), jnp.float32)],
        compiler_params=pltpu.CompilerParams(vmem_limit_bytes=16 * MIB),
        name="combine",
    )(side, slots, weights, back)


def last_kernel(side_ref, own_ref, other_ref, keep_ref, got_ref, out_ref, sums_ref):
    tokens, width = out_ref.shape
    half = width // LANES
    side = side_ref[0]
    for t in range(tokens):
        at = pl.multiple_of((2 * t + side) * half, half)
        rows = slice(t * half, (t + 1) * half)
        hidden = own_ref[pl.ds(at, half), :] + other_ref[pl.ds(at, half), :]
        sums_ref[rows, :] = hidden + (keep_ref[rows, :] + got_ref[rows, :])
    for f in range(half):
        out_ref[:, f * LANES : (f + 1) * LANES] = sums_ref[
            pl.ds(f, tokens, stride=half), :
        ].astype(jnp.bfloat16)


def last_call(side, own, other, keep, got, tokens):
    vmem = pl.BlockSpec(memory_space=pltpu.VMEM)
    return pl.pallas_call(
        last_kernel,
        out_shape=jax.ShapeDtypeStruct((tokens, keep.size // tokens), jnp.bfloat16),
        in_specs=[pl.BlockSpec(memory_space=pltpu.SMEM), vmem, vmem, vmem, vmem],
        out_specs=vmem,
        scratch_shapes=[pltpu.VMEM(keep.shape, jnp.float32)],
        compiler_params=pltpu.CompilerParams(vmem_limit_bytes=16 * MIB),
        name="last",
    )(side, own, other, keep, got)


def slot_tables(route_ids, route_weight, side_index, per_side, experts):
    tokens, top = route_ids.shape
    entries = tokens * top
    ids = route_ids.reshape(-1)
    token = lax.broadcasted_iota(jnp.int32, (tokens, top), 0).reshape(-1)
    same = (ids[:, None] == ids[None, :]) & (token[:, None] > token[None, :])
    position = jnp.sum(same.astype(jnp.int32), axis=1)
    local = ids - side_index * per_side
    on_side = (local >= 0) & (local < per_side)
    slot = jnp.where(on_side, local * CAP + position, -1)
    weights = jnp.where(on_side, route_weight.reshape(-1), 0.0)
    hit = slot[None, :] == lax.broadcasted_iota(jnp.int32, (per_side * CAP, entries), 0)
    source = tokens - jnp.sum(jnp.where(hit, tokens - token[None, :], 0), axis=1)
    return source, jnp.maximum(slot, 0), weights


def body(
    query,
    key_in,
    value,
    out_gate,
    decay_arg,
    beta_arg,
    decay_log,
    step_bias,
    states,
    norm_gain,
    out_weight,
    residual,
    post_gain,
    route_ids,
    route_weight,
    w_gate,
    w_up,
    w_down,
):
    tokens, width = residual.shape
    blocks = width // LANES
    dev_count = lax.axis_size("dev")
    experts = w_gate.shape[0]
    side_index = lax.axis_index("side")
    side = side_index.reshape(1)
    swap = [(0, 1), (1, 0)]
    own = delta_call(
        side,
        query,
        key_in,
        value,
        out_gate,
        decay_arg.T,
        beta_arg.T,
        decay_log.reshape(1, -1),
        step_bias.reshape(1, -1),
        states,
        norm_gain.reshape(1, -1),
        residual,
        out_weight,
    )
    other = lax.ppermute(own, "side", swap)
    source, slots, weights = slot_tables(
        route_ids, route_weight, side_index, dev_count * experts, experts
    )
    send_rows = pack_call(source, own, other, post_gain.reshape(blocks, LANES))
    received = lax.all_to_all(send_rows, "dev", split_axis=0, concat_axis=0, tiled=True)
    expert_out = expert_call(
        received.reshape(dev_count, -1, LANES), w_gate, w_up, w_down
    ).reshape(received.shape)
    back = lax.all_to_all(expert_out, "dev", split_axis=0, concat_axis=0, tiled=True)
    keep, send = gather_call(side, slots, weights, back, tokens, blocks)
    got = lax.ppermute(send, "side", swap)
    return last_call(side, own, other, keep, got, tokens)


def solution(mesh):
    in_specs = (
        P("dev", "side", None),
        P("dev", "side", None),
        P("dev", "side", None),
        P("dev", "side", None),
        P("dev", "side"),
        P("dev", "side"),
        P("side"),
        P("side"),
        P("dev", "side", None, None),
        P(),
        P("side", None),
        P("dev", None),
        P(),
        P("dev", None),
        P("dev", None),
        P(("side", "dev"), None, None),
        P(("side", "dev"), None, None),
        P(("side", "dev"), None, None),
    )
    out_specs = P("dev", "side")
    return jax.shard_map(body, mesh=mesh, in_specs=in_specs, out_specs=out_specs, check_vma=False)
```

```python
import jax
import jax.numpy as jnp
from jax import lax
from jax.experimental import pallas as pl
from jax.experimental.pallas import tpu as pltpu
from jax.sharding import PartitionSpec as P

CAP = 3
EPSILON = 1e-06
LANES = 128
TILE = 16
STEP_TOKENS = 2
MIB = 1 << 20


def in_hbm(*arrays):
    return [pltpu.with_memory_space_constraint(a, pltpu.HBM) for a in arrays]


def softplus(x):
    return jnp.maximum(x, 0.0) + jnp.log1p(jnp.exp(-jnp.abs(x)))


def sigmoid(x):
    return 1.0 / (1.0 + jnp.exp(-x))


def unit_rows(source):
    return source * lax.rsqrt(jnp.sum(source * source, -1, keepdims=True) + EPSILON)


def row_to_column(row):
    n = row.shape[1]
    square = jnp.broadcast_to(row, (n, n))
    on_diagonal = lax.broadcasted_iota(jnp.int32, (n, n), 0) == lax.broadcasted_iota(
        jnp.int32, (n, n), 1
    )
    return jnp.sum(jnp.where(on_diagonal, square, 0.0), axis=1, keepdims=True)


def delta_kernel(
    side_ref,
    query_ref,
    key_ref,
    value_ref,
    gate_ref,
    decay_ref,
    beta_ref,
    log_ref,
    bias_ref,
    gain_ref,
    residual_ref,
    state_hbm,
    weight_hbm,
    out_ref,
    state_ref,
    weight_ref,
    qstate_ref,
    kstate_ref,
    heads_ref,
    state_sem,
    weight_sem,
):
    tokens, width = residual_ref.shape
    heads = value_ref.shape[1]
    key_heads = query_ref.shape[1]
    repeats = heads // key_heads
    size = query_ref.shape[2]
    parts = tokens // STEP_TOKENS
    loads = [
        pltpu.make_async_copy(
            state_hbm.at[pl.ds(i * STEP_TOKENS, STEP_TOKENS)],
            state_ref.at[pl.ds(i * STEP_TOKENS, STEP_TOKENS)],
            state_sem.at[i],
        )
        for i in range(parts)
    ]
    for load in loads:
        load.start()
    weight_load = pltpu.make_async_copy(weight_hbm, weight_ref, weight_sem)
    weight_load.start()

    def rows(ref):
        return jnp.concatenate([ref[t].astype(jnp.float32) for t in range(tokens)], 0)

    query_unit = unit_rows(rows(query_ref)) * size ** (-0.5)
    key_unit = unit_rows(rows(key_ref))
    count = tokens * key_heads
    columns = jnp.concatenate([query_unit, key_unit], 0).T
    products = jnp.broadcast_to(
        jnp.sum(query_unit * key_unit, -1, keepdims=True), (count, size)
    )
    for r in range(repeats):
        heads_ref[pl.ds(r, count, stride=repeats), :] = products
    retain_all = jnp.exp(
        -jnp.exp(row_to_column(log_ref[...]))
        * softplus(decay_ref[...] + row_to_column(bias_ref[...]))
    )
    rate_all = sigmoid(beta_ref[...])
    for i in range(parts):
        loads[i].wait()
        for t in range(i * STEP_TOKENS, (i + 1) * STEP_TOKENS):
            for k in range(key_heads):
                at = t * key_heads + k
                qcol = jnp.broadcast_to(columns[:, at : at + 1], (size, size))
                at = at + count
                kcol = jnp.broadcast_to(columns[:, at : at + 1], (size, size))
                for r in range(repeats):
                    h = k * repeats + r
                    state = state_ref[t, h]
                    at = t * heads + h
                    qstate_ref[at : at + 1, :] = jnp.sum(qcol * state, axis=0, keepdims=True)
                    kstate_ref[at : at + 1, :] = jnp.sum(kcol * state, axis=0, keepdims=True)

    def per_head(table):
        return jnp.concatenate(
            [jnp.broadcast_to(table[:, t : t + 1], (heads, size)) for t in range(tokens)], 0
        )

    retain, rate = per_head(retain_all), per_head(rate_all)
    correct = rate * (rows(value_ref) - retain * kstate_ref[...])
    attend = retain * qstate_ref[...] + heads_ref[...] * correct
    inv_rms = lax.rsqrt(jnp.mean(attend * attend, -1, keepdims=True) + EPSILON)
    gate = rows(gate_ref)
    heads_ref[...] = attend * inv_rms * gain_ref[...] * (gate * sigmoid(gate))
    gated_out = jnp.concatenate(
        [heads_ref[pl.ds(h, tokens, stride=heads), :] for h in range(heads)], 1
    ).astype(jnp.bfloat16)
    weight_load.wait()
    side = side_ref[0]
    blocks = width // LANES
    wide = 4 * LANES
    for n in range(width // wide):
        part = jnp.dot(
            gated_out,
            weight_ref[:, n * wide : (n + 1) * wide],
            preferred_element_type=jnp.float32,
        )
        kept = residual_ref[:, n * wide : (n + 1) * wide].astype(jnp.float32)
        part = part + jnp.where(side == 0, kept, 0.0)
        for f in range(4):
            out_ref[pl.ds(n * 4 + f, tokens, stride=blocks), :] = part[
                :, f * LANES : (f + 1) * LANES
            ]


def delta_call(side, query, key_in, value, gate, decay, beta, log, bias, states, gain, residual, weight):
    tokens, heads, size = value.shape
    width = residual.shape[1]
    small = (query, key_in, value, gate, decay, beta, log, bias, gain, residual)

    def whole(array):
        return pl.BlockSpec(array.shape, lambda i: (0,) * array.ndim)

    pairs = pltpu.VMEM((tokens * heads, size), jnp.float32)
    return pl.pallas_call(
        delta_kernel,
        grid=(1,),
        out_shape=jax.ShapeDtypeStruct((tokens * width // LANES, LANES), jnp.float32),
        in_specs=[pl.BlockSpec(memory_space=pltpu.SMEM)]
        + [whole(a) for a in small]
        + [pl.BlockSpec(memory_space=pl.ANY)] * 2,
        out_specs=pl.BlockSpec((tokens * width // LANES, LANES), lambda i: (0, 0)),
        scratch_shapes=[
            pltpu.VMEM(states.shape, states.dtype),
            pltpu.VMEM(weight.shape, weight.dtype),
            pairs,
            pairs,
            pairs,
            pltpu.SemaphoreType.DMA((tokens // STEP_TOKENS,)),
            pltpu.SemaphoreType.DMA,
        ],
        compiler_params=pltpu.CompilerParams(vmem_limit_bytes=24 * MIB),
        name="delta",
    )(side, *in_hbm(*small, states, weight))


def pack_kernel(source_ref, own_ref, other_ref, gain_ref, out_ref, tiles_ref):
    blocks = gain_ref.shape[0]
    tokens = own_ref.shape[0] // blocks
    for t in range(tokens):
        rows = slice(t * blocks, (t + 1) * blocks)
        hidden = own_ref[rows, :] + other_ref[rows, :]
        mean = jnp.sum(
            jnp.sum(hidden * hidden, axis=0, keepdims=True), axis=1, keepdims=True
        ) * (1.0 / (blocks * LANES))
        tiles_ref[rows, :] = (hidden * lax.rsqrt(mean + EPSILON) * gain_ref[...]).astype(
            jnp.bfloat16
        )
    tiles_ref[tokens * blocks :, :] = jnp.zeros((blocks, LANES), jnp.bfloat16)
    slots = out_ref.shape[0] // blocks
    for s in range(slots):
        at = pl.multiple_of(source_ref[s] * blocks, blocks)
        out_ref[s * blocks : (s + 1) * blocks, :] = tiles_ref[pl.ds(at, blocks), :]


def pack_call(source, own, other, gain):
    blocks = gain.shape[0]
    slots = source.shape[0]
    vmem = pl.BlockSpec(memory_space=pltpu.VMEM)
    return pl.pallas_call(
        pack_kernel,
        out_shape=jax.ShapeDtypeStruct((slots * blocks, LANES), jnp.bfloat16),
        in_specs=[pl.BlockSpec(memory_space=pltpu.SMEM), vmem, vmem, vmem],
        out_specs=vmem,
        scratch_shapes=[pltpu.VMEM((own.shape[0] + blocks, LANES), jnp.bfloat16)],
        compiler_params=pltpu.CompilerParams(vmem_limit_bytes=16 * MIB),
        name="pack",
    )(source, own, other, gain)


def expert_kernel(
    x_ref, gate_hbm, up_hbm, down_hbm, out_ref, gate_ref, up_ref, down_ref, rows_ref, sems
):
    experts, width, units = gate_hbm.shape
    sources = x_ref.shape[0]
    blocks = width // LANES
    groups = sources // TILE
    copies = []
    for e in range(experts):
        for i, (hbm, ref) in enumerate(
            ((gate_hbm, gate_ref), (up_hbm, up_ref), (down_hbm, down_ref))
        ):
            copies.append(pltpu.make_async_copy(hbm.at[e], ref.at[e], sems.at[e, i]))
            copies[-1].start()
    row = lax.broadcasted_iota(jnp.int32, (TILE * blocks, TILE * blocks), 0)
    column = lax.broadcasted_iota(jnp.int32, (TILE * blocks, TILE * blocks), 1)
    swap = jnp.where((row % TILE) * TILE + row // TILE == column, 1.0, 0.0).astype(jnp.bfloat16)
    for e in range(experts):
        for g in range(groups):
            for c in range(CAP):
                at = (e * CAP + c) * blocks
                block = x_ref[g * TILE : (g + 1) * TILE, at : at + blocks, :]
                block = block.reshape(TILE * blocks, LANES)
                turned = jnp.dot(swap, block, preferred_element_type=jnp.float32)
                turned = turned.astype(jnp.bfloat16)
                r = ((e * groups + g) * CAP + c) * TILE
                for f in range(blocks):
                    rows_ref[r : r + TILE, f * LANES : (f + 1) * LANES] = turned[
                        f * TILE : (f + 1) * TILE
                    ]
    count = groups * CAP * TILE
    for e in range(experts):
        x = rows_ref[e * count : (e + 1) * count, :]
        copies[3 * e].wait()
        gate = jnp.dot(x, gate_ref[e], preferred_element_type=jnp.float32)
        copies[3 * e + 1].wait()
        up = jnp.dot(x, up_ref[e], preferred_element_type=jnp.float32)
        inner = (gate * sigmoid(gate) * up).astype(jnp.bfloat16)
        copies[3 * e + 2].wait()
        wide = 4 * LANES
        for n in range(width // wide):
            y = jnp.dot(
                inner, down_ref[e, :, n * wide : (n + 1) * wide], preferred_element_type=jnp.float32
            )
            rows_ref[e * count : (e + 1) * count, n * wide : (n + 1) * wide] = y.astype(
                jnp.bfloat16
            )
        for g in range(groups):
            for c in range(CAP):
                r = ((e * groups + g) * CAP + c) * TILE
                block = jnp.concatenate(
                    [
                        rows_ref[r : r + TILE, f * LANES : (f + 1) * LANES]
                        for f in range(blocks)
                    ],
                    0,
                )
                turned = jnp.dot(swap, block, preferred_element_type=jnp.float32)
                at = (e * CAP + c) * blocks
                out_ref[g * TILE : (g + 1) * TILE, at : at + blocks, :] = turned.astype(
                    jnp.bfloat16
                ).reshape(TILE, blocks, LANES)


def expert_call(received, w_gate, w_up, w_down):
    experts, width, units = w_gate.shape
    vmem = pl.BlockSpec(memory_space=pltpu.VMEM)
    hbm = pl.BlockSpec(memory_space=pl.ANY)
    slots = received.shape[0] * CAP * experts
    return pl.pallas_call(
        expert_kernel,
        out_shape=jax.ShapeDtypeStruct(received.shape, received.dtype),
        in_specs=[vmem, hbm, hbm, hbm],
        out_specs=vmem,
        scratch_shapes=[
            pltpu.VMEM(w_gate.shape, w_gate.dtype),
            pltpu.VMEM(w_up.shape, w_up.dtype),
            pltpu.VMEM(w_down.shape, w_down.dtype),
            pltpu.VMEM((slots, width), jnp.bfloat16),
            pltpu.SemaphoreType.DMA((experts, 3)),
        ],
        compiler_params=pltpu.CompilerParams(vmem_limit_bytes=32 * MIB),
        name="experts",
    )(received, *in_hbm(w_gate, w_up, w_down))


def gather_kernel(side_ref, slot_ref, weight_ref, back_ref, keep_ref, send_ref, sums_ref):
    blocks = sums_ref.shape[0]
    half = blocks // 2
    tokens = keep_ref.shape[0] // half
    top = slot_ref.shape[0] // tokens
    side = side_ref[0]
    for t in range(tokens):
        total = jnp.zeros((blocks, LANES), jnp.float32)
        for k in range(top):
            at = pl.multiple_of(slot_ref[t * top + k] * blocks, blocks)
            tile = back_ref[pl.ds(at, blocks), :].astype(jnp.float32)
            total = total + weight_ref[t * top + k] * tile
        sums_ref[...] = total
        own = pl.multiple_of(side * half, half)
        other = pl.multiple_of((1 - side) * half, half)
        keep_ref[t * half : (t + 1) * half, :] = sums_ref[pl.ds(own, half), :]
        send_ref[t * half : (t + 1) * half, :] = sums_ref[pl.ds(other, half), :]


def gather_call(side, slots, weights, back, tokens, blocks):
    vmem = pl.BlockSpec(memory_space=pltpu.VMEM)
    smem = pl.BlockSpec(memory_space=pltpu.SMEM)
    half = jax.ShapeDtypeStruct((tokens * blocks // 2, LANES), jnp.float32)
    return pl.pallas_call(
        gather_kernel,
        out_shape=(half, half),
        in_specs=[smem, smem, smem, vmem],
        out_specs=(vmem, vmem),
        scratch_shapes=[pltpu.VMEM((blocks, LANES), jnp.float32)],
        compiler_params=pltpu.CompilerParams(vmem_limit_bytes=16 * MIB),
        name="combine",
    )(side, slots, weights, back)


def last_kernel(side_ref, own_ref, other_ref, keep_ref, got_ref, out_ref, sums_ref):
    tokens, width = out_ref.shape
    half = width // LANES
    side = side_ref[0]
    for t in range(tokens):
        at = pl.multiple_of((2 * t + side) * half, half)
        rows = slice(t * half, (t + 1) * half)
        hidden = own_ref[pl.ds(at, half), :] + other_ref[pl.ds(at, half), :]
        sums_ref[rows, :] = hidden + (keep_ref[rows, :] + got_ref[rows, :])
    for f in range(half):
        out_ref[:, f * LANES : (f + 1) * LANES] = sums_ref[
            pl.ds(f, tokens, stride=half), :
        ].astype(jnp.bfloat16)


def last_call(side, own, other, keep, got, tokens):
    vmem = pl.BlockSpec(memory_space=pltpu.VMEM)
    return pl.pallas_call(
        last_kernel,
        out_shape=jax.ShapeDtypeStruct((tokens, keep.size // tokens), jnp.bfloat16),
        in_specs=[pl.BlockSpec(memory_space=pltpu.SMEM), vmem, vmem, vmem, vmem],
        out_specs=vmem,
        scratch_shapes=[pltpu.VMEM(keep.shape, jnp.float32)],
        compiler_params=pltpu.CompilerParams(vmem_limit_bytes=16 * MIB),
        name="last",
    )(side, own, other, keep, got)


def slot_tables(route_ids, route_weight, side_index, per_side, experts):
    tokens, top = route_ids.shape
    entries = tokens * top
    ids = route_ids.reshape(-1)
    token = lax.broadcasted_iota(jnp.int32, (tokens, top), 0).reshape(-1)
    same = (ids[:, None] == ids[None, :]) & (token[:, None] > token[None, :])
    position = jnp.sum(same.astype(jnp.int32), axis=1)
    local = ids - side_index * per_side
    on_side = (local >= 0) & (local < per_side)
    dev = local // experts
    place = jnp.where(side_index == 0, dev, per_side // experts - 1 - dev)
    slot = jnp.where(on_side, (place * experts + local % experts) * CAP + position, -1)
    weights = jnp.where(on_side, route_weight.reshape(-1), 0.0)
    hit = slot[None, :] == lax.broadcasted_iota(jnp.int32, (per_side * CAP, entries), 0)
    source = tokens - jnp.sum(jnp.where(hit, tokens - token[None, :], 0), axis=1)
    return source, jnp.maximum(slot, 0), weights


def exchange(rows, dev_count):
    ahead = list(range(dev_count))
    groups = [ahead, [dev_count + d for d in reversed(ahead)]]
    return lax.all_to_all(
        rows,
        ("side", "dev"),
        split_axis=0,
        concat_axis=0,
        axis_index_groups=groups,
        tiled=True,
    )


def body(
    query,
    key_in,
    value,
    out_gate,
    decay_arg,
    beta_arg,
    decay_log,
    step_bias,
    states,
    norm_gain,
    out_weight,
    residual,
    post_gain,
    route_ids,
    route_weight,
    w_gate,
    w_up,
    w_down,
):
    tokens, width = residual.shape
    blocks = width // LANES
    dev_count = lax.axis_size("dev")
    experts = w_gate.shape[0]
    side_index = lax.axis_index("side")
    side = side_index.reshape(1)
    swap = [(0, 1), (1, 0)]
    own = delta_call(
        side,
        query,
        key_in,
        value,
        out_gate,
        decay_arg.T,
        beta_arg.T,
        decay_log.reshape(1, -1),
        step_bias.reshape(1, -1),
        states,
        norm_gain.reshape(1, -1),
        residual,
        out_weight,
    )
    other = lax.ppermute(own, "side", swap)
    source, slots, weights = slot_tables(
        route_ids, route_weight, side_index, dev_count * experts, experts
    )
    send_rows = pack_call(source, own, other, post_gain.reshape(blocks, LANES))
    received = exchange(send_rows, dev_count)
    expert_out = expert_call(
        received.reshape(dev_count, -1, LANES), w_gate, w_up, w_down
    ).reshape(received.shape)
    back = exchange(expert_out, dev_count)
    keep, send = gather_call(side, slots, weights, back, tokens, blocks)
    got = lax.ppermute(send, "side", swap)
    return last_call(side, own, other, keep, got, tokens)


def solution(mesh):
    in_specs = (
        P("dev", "side", None),
        P("dev", "side", None),
        P("dev", "side", None),
        P("dev", "side", None),
        P("dev", "side"),
        P("dev", "side"),
        P("side"),
        P("side"),
        P("dev", "side", None, None),
        P(),
        P("side", None),
        P("dev", None),
        P(),
        P("dev", None),
        P("dev", None),
        P(("side", "dev"), None, None),
        P(("side", "dev"), None, None),
        P(("side", "dev"), None, None),
    )
    out_specs = P("dev", "side")
    return jax.shard_map(body, mesh=mesh, in_specs=in_specs, out_specs=out_specs, check_vma=False)
```

```python
import jax
import jax.numpy as jnp
from jax import lax
from jax.experimental import pallas as pl
from jax.experimental.pallas import tpu as pltpu
from jax.sharding import PartitionSpec as P

CAP = 3
EPSILON = 1e-06
LANES = 128
TILE = 16
STEP_TOKENS = 2
MIB = 1 << 20


def in_hbm(*arrays):
    return [pltpu.with_memory_space_constraint(a, pltpu.HBM) for a in arrays]


def softplus(x):
    return jnp.maximum(x, 0.0) + jnp.log1p(jnp.exp(-jnp.abs(x)))


def sigmoid(x):
    return 1.0 / (1.0 + jnp.exp(-x))


def unit_rows(source):
    return source * lax.rsqrt(jnp.sum(source * source, -1, keepdims=True) + EPSILON)


def row_to_column(row):
    n = row.shape[1]
    square = jnp.broadcast_to(row, (n, n))
    on_diagonal = lax.broadcasted_iota(jnp.int32, (n, n), 0) == lax.broadcasted_iota(
        jnp.int32, (n, n), 1
    )
    return jnp.sum(jnp.where(on_diagonal, square, 0.0), axis=1, keepdims=True)


def delta_kernel(side_ref, *refs):
    small_hbm, state_hbm, weight_hbm, out_ref = refs[:10], refs[10], refs[11], refs[12]
    small_refs, refs = refs[13:23], refs[23:]
    state_ref, weight_ref, qstate_ref, kstate_ref, heads_ref, small_sem, state_sem, weight_sem = refs
    query_ref, key_ref, value_ref, gate_ref, decay_ref = small_refs[:5]
    beta_ref, log_ref, bias_ref, gain_ref, residual_ref = small_refs[5:]
    tokens, width = residual_ref.shape
    heads = value_ref.shape[1]
    key_heads = query_ref.shape[1]
    repeats = heads // key_heads
    size = query_ref.shape[2]
    parts = tokens // STEP_TOKENS
    smalls = [
        pltpu.make_async_copy(source, target, small_sem.at[i])
        for i, (source, target) in enumerate(zip(small_hbm, small_refs))
    ]
    loads = [
        pltpu.make_async_copy(
            state_hbm.at[pl.ds(i * STEP_TOKENS, STEP_TOKENS)],
            state_ref.at[pl.ds(i * STEP_TOKENS, STEP_TOKENS)],
            state_sem.at[i],
        )
        for i in range(parts)
    ]
    weight_load = pltpu.make_async_copy(weight_hbm, weight_ref, weight_sem)
    for load in smalls[:2] + loads[:2] + smalls[2:] + loads[2:] + [weight_load]:
        load.start()
    for load in smalls[:2]:
        load.wait()

    def rows(ref):
        return jnp.concatenate([ref[t].astype(jnp.float32) for t in range(tokens)], 0)

    query_unit = unit_rows(rows(query_ref)) * size ** (-0.5)
    key_unit = unit_rows(rows(key_ref))
    count = tokens * key_heads
    columns = jnp.concatenate([query_unit, key_unit], 0).T
    products = jnp.broadcast_to(
        jnp.sum(query_unit * key_unit, -1, keepdims=True), (count, size)
    )
    for r in range(repeats):
        heads_ref[pl.ds(r, count, stride=repeats), :] = products
    for i in range(parts):
        loads[i].wait()
        for t in range(i * STEP_TOKENS, (i + 1) * STEP_TOKENS):
            for k in range(key_heads):
                at = t * key_heads + k
                qcol = jnp.broadcast_to(columns[:, at : at + 1], (size, size))
                at = at + count
                kcol = jnp.broadcast_to(columns[:, at : at + 1], (size, size))
                for r in range(repeats):
                    h = k * repeats + r
                    state = state_ref[t, h]
                    at = t * heads + h
                    qstate_ref[at : at + 1, :] = jnp.sum(qcol * state, axis=0, keepdims=True)
                    kstate_ref[at : at + 1, :] = jnp.sum(kcol * state, axis=0, keepdims=True)

    for load in smalls[2:]:
        load.wait()
    retain_all = jnp.exp(
        -jnp.exp(row_to_column(log_ref[...]))
        * softplus(decay_ref[...] + row_to_column(bias_ref[...]))
    )
    rate_all = sigmoid(beta_ref[...])

    def per_head(table):
        return jnp.concatenate(
            [jnp.broadcast_to(table[:, t : t + 1], (heads, size)) for t in range(tokens)], 0
        )

    retain, rate = per_head(retain_all), per_head(rate_all)
    correct = rate * (rows(value_ref) - retain * kstate_ref[...])
    attend = retain * qstate_ref[...] + heads_ref[...] * correct
    inv_rms = lax.rsqrt(jnp.mean(attend * attend, -1, keepdims=True) + EPSILON)
    gate = rows(gate_ref)
    heads_ref[...] = attend * inv_rms * gain_ref[...] * (gate * sigmoid(gate))
    gated_out = jnp.concatenate(
        [heads_ref[pl.ds(h, tokens, stride=heads), :] for h in range(heads)], 1
    ).astype(jnp.bfloat16)
    weight_load.wait()
    side = side_ref[0]
    blocks = width // LANES
    wide = 4 * LANES
    for n in range(width // wide):
        part = jnp.dot(
            gated_out,
            weight_ref[:, n * wide : (n + 1) * wide],
            preferred_element_type=jnp.float32,
        )
        kept = residual_ref[:, n * wide : (n + 1) * wide].astype(jnp.float32)
        part = part + jnp.where(side == 0, kept, 0.0)
        for f in range(4):
            out_ref[pl.ds(n * 4 + f, tokens, stride=blocks), :] = part[
                :, f * LANES : (f + 1) * LANES
            ]


def delta_call(side, query, key_in, value, gate, decay, beta, log, bias, states, gain, residual, weight):
    tokens, heads, size = value.shape
    width = residual.shape[1]
    small = (query, key_in, value, gate, decay, beta, log, bias, gain, residual)
    vmem = pl.BlockSpec(memory_space=pltpu.VMEM)
    pairs = pltpu.VMEM((tokens * heads, size), jnp.float32)
    return pl.pallas_call(
        delta_kernel,
        out_shape=jax.ShapeDtypeStruct((tokens * width // LANES, LANES), jnp.float32),
        in_specs=[pl.BlockSpec(memory_space=pltpu.SMEM)]
        + [pl.BlockSpec(memory_space=pl.ANY)] * (len(small) + 2),
        out_specs=vmem,
        scratch_shapes=[pltpu.VMEM(a.shape, a.dtype) for a in small]
        + [
            pltpu.VMEM(states.shape, states.dtype),
            pltpu.VMEM(weight.shape, weight.dtype),
            pairs,
            pairs,
            pairs,
            pltpu.SemaphoreType.DMA((len(small),)),
            pltpu.SemaphoreType.DMA((tokens // STEP_TOKENS,)),
            pltpu.SemaphoreType.DMA,
        ],
        compiler_params=pltpu.CompilerParams(vmem_limit_bytes=24 * MIB),
        name="delta",
    )(side, *in_hbm(*small, states, weight))


def pack_kernel(source_ref, own_ref, other_ref, gain_ref, out_ref, tiles_ref):
    blocks = gain_ref.shape[0]
    tokens = own_ref.shape[0] // blocks
    for t in range(tokens):
        rows = slice(t * blocks, (t + 1) * blocks)
        hidden = own_ref[rows, :] + other_ref[rows, :]
        mean = jnp.sum(
            jnp.sum(hidden * hidden, axis=0, keepdims=True), axis=1, keepdims=True
        ) * (1.0 / (blocks * LANES))
        tiles_ref[rows, :] = (hidden * lax.rsqrt(mean + EPSILON) * gain_ref[...]).astype(
            jnp.bfloat16
        )
    tiles_ref[tokens * blocks :, :] = jnp.zeros((blocks, LANES), jnp.bfloat16)
    slots = out_ref.shape[0] // blocks
    for s in range(slots):
        at = pl.multiple_of(source_ref[s] * blocks, blocks)
        out_ref[s * blocks : (s + 1) * blocks, :] = tiles_ref[pl.ds(at, blocks), :]


def pack_call(source, own, other, gain):
    blocks = gain.shape[0]
    slots = source.shape[0]
    vmem = pl.BlockSpec(memory_space=pltpu.VMEM)
    return pl.pallas_call(
        pack_kernel,
        out_shape=jax.ShapeDtypeStruct((slots * blocks, LANES), jnp.bfloat16),
        in_specs=[pl.BlockSpec(memory_space=pltpu.SMEM), vmem, vmem, vmem],
        out_specs=vmem,
        scratch_shapes=[pltpu.VMEM((own.shape[0] + blocks, LANES), jnp.bfloat16)],
        compiler_params=pltpu.CompilerParams(vmem_limit_bytes=16 * MIB),
        name="pack",
    )(source, own, other, gain)


def expert_kernel(x_ref, gate_ref, up_hbm, down_hbm, out_ref, up_ref, down_ref, rows_ref, sems):
    experts, width, units = gate_ref.shape
    sources = x_ref.shape[0]
    blocks = width // LANES
    groups = sources // TILE
    count = groups * CAP * TILE
    wide = 4 * LANES
    copies = []
    for e in range(experts):
        copies.append(pltpu.make_async_copy(up_hbm.at[e], up_ref.at[e], sems.at[2 * e]))
        copies.append(pltpu.make_async_copy(down_hbm.at[e], down_ref.at[e], sems.at[2 * e + 1]))
    for copy in copies[:2]:
        copy.start()
    row = lax.broadcasted_iota(jnp.int32, (TILE * blocks, TILE * blocks), 0)
    column = lax.broadcasted_iota(jnp.int32, (TILE * blocks, TILE * blocks), 1)
    swap = jnp.where((row % TILE) * TILE + row // TILE == column, 1.0, 0.0).astype(jnp.bfloat16)
    places = [(g, c) for g in range(groups) for c in range(CAP)]

    def turn(pair):
        turned = jnp.dot(swap, jnp.concatenate(pair, 1), preferred_element_type=jnp.float32)
        turned = turned.astype(jnp.bfloat16)
        return turned[:, :LANES], turned[:, LANES:]

    def place_of(e, g, c):
        return g * TILE, (e * CAP + c) * blocks

    for e in range(experts):
        for n in range(0, len(places), 2):
            pair = []
            for g, c in places[n : n + 2]:
                top, at = place_of(e, g, c)
                block = x_ref[top : top + TILE, at : at + blocks, :]
                pair.append(block.reshape(TILE * blocks, LANES))
            for i, turned in enumerate(turn(pair)):
                r = e * count + (n + i) * TILE
                for f in range(blocks):
                    rows_ref[r : r + TILE, f * LANES : (f + 1) * LANES] = turned[
                        f * TILE : (f + 1) * TILE
                    ]
        x = rows_ref[e * count : (e + 1) * count, :]
        gate = jnp.dot(x, gate_ref[e], preferred_element_type=jnp.float32)
        copies[2 * e].wait()
        if e + 1 < experts:
            copies[2 * e + 2].start()
        up = jnp.dot(x, up_ref[e], preferred_element_type=jnp.float32)
        inner = (gate * sigmoid(gate) * up).astype(jnp.bfloat16)
        copies[2 * e + 1].wait()
        if e + 1 < experts:
            copies[2 * e + 3].start()
        for n in range(width // wide):
            y = jnp.dot(
                inner, down_ref[e, :, n * wide : (n + 1) * wide], preferred_element_type=jnp.float32
            )
            rows_ref[e * count : (e + 1) * count, n * wide : (n + 1) * wide] = y.astype(
                jnp.bfloat16
            )
        for n in range(0, len(places), 2):
            pair = []
            for i in range(2):
                r = e * count + (n + i) * TILE
                pair.append(
                    jnp.concatenate(
                        [
                            rows_ref[r : r + TILE, f * LANES : (f + 1) * LANES]
                            for f in range(blocks)
                        ],
                        0,
                    )
                )
            for (g, c), turned in zip(places[n : n + 2], turn(pair)):
                top, at = place_of(e, g, c)
                out_ref[top : top + TILE, at : at + blocks, :] = turned.reshape(
                    TILE, blocks, LANES
                )


def expert_call(received, w_gate, w_up, w_down):
    experts, width, units = w_gate.shape
    vmem = pl.BlockSpec(memory_space=pltpu.VMEM)
    hbm = pl.BlockSpec(memory_space=pl.ANY)
    slots = received.shape[0] * CAP * experts
    return pl.pallas_call(
        expert_kernel,
        out_shape=jax.ShapeDtypeStruct(received.shape, received.dtype),
        in_specs=[vmem, vmem, hbm, hbm],
        out_specs=vmem,
        scratch_shapes=[
            pltpu.VMEM(w_up.shape, w_up.dtype),
            pltpu.VMEM(w_down.shape, w_down.dtype),
            pltpu.VMEM((slots, width), jnp.bfloat16),
            pltpu.SemaphoreType.DMA((2 * experts,)),
        ],
        compiler_params=pltpu.CompilerParams(vmem_limit_bytes=24 * MIB),
        name="experts",
    )(received, w_gate, *in_hbm(w_up, w_down))


def gather_kernel(side_ref, slot_ref, weight_ref, back_ref, keep_ref, send_ref, sums_ref):
    blocks = sums_ref.shape[0]
    half = blocks // 2
    tokens = keep_ref.shape[0] // half
    top = slot_ref.shape[0] // tokens
    side = side_ref[0]
    for t in range(tokens):
        total = jnp.zeros((blocks, LANES), jnp.float32)
        for k in range(top):
            at = pl.multiple_of(slot_ref[t * top + k] * blocks, blocks)
            tile = back_ref[pl.ds(at, blocks), :].astype(jnp.float32)
            total = total + weight_ref[t * top + k] * tile
        sums_ref[...] = total
        own = pl.multiple_of(side * half, half)
        other = pl.multiple_of((1 - side) * half, half)
        keep_ref[t * half : (t + 1) * half, :] = sums_ref[pl.ds(own, half), :]
        send_ref[t * half : (t + 1) * half, :] = sums_ref[pl.ds(other, half), :]


def gather_call(side, slots, weights, back, tokens, blocks):
    vmem = pl.BlockSpec(memory_space=pltpu.VMEM)
    smem = pl.BlockSpec(memory_space=pltpu.SMEM)
    half = jax.ShapeDtypeStruct((tokens * blocks // 2, LANES), jnp.float32)
    return pl.pallas_call(
        gather_kernel,
        out_shape=(half, half),
        in_specs=[smem, smem, smem, vmem],
        out_specs=(vmem, vmem),
        scratch_shapes=[pltpu.VMEM((blocks, LANES), jnp.float32)],
        compiler_params=pltpu.CompilerParams(vmem_limit_bytes=16 * MIB),
        name="combine",
    )(side, slots, weights, back)


def last_kernel(side_ref, own_ref, other_ref, keep_ref, got_ref, out_ref, sums_ref):
    tokens, width = out_ref.shape
    half = width // LANES
    side = side_ref[0]
    for t in range(tokens):
        at = pl.multiple_of((2 * t + side) * half, half)
        rows = slice(t * half, (t + 1) * half)
        hidden = own_ref[pl.ds(at, half), :] + other_ref[pl.ds(at, half), :]
        sums_ref[rows, :] = hidden + (keep_ref[rows, :] + got_ref[rows, :])
    for f in range(half):
        out_ref[:, f * LANES : (f + 1) * LANES] = sums_ref[
            pl.ds(f, tokens, stride=half), :
        ].astype(jnp.bfloat16)


def last_call(side, own, other, keep, got, tokens):
    vmem = pl.BlockSpec(memory_space=pltpu.VMEM)
    return pl.pallas_call(
        last_kernel,
        out_shape=jax.ShapeDtypeStruct((tokens, keep.size // tokens), jnp.bfloat16),
        in_specs=[pl.BlockSpec(memory_space=pltpu.SMEM), vmem, vmem, vmem, vmem],
        out_specs=vmem,
        scratch_shapes=[pltpu.VMEM(keep.shape, jnp.float32)],
        compiler_params=pltpu.CompilerParams(vmem_limit_bytes=16 * MIB),
        name="last",
    )(side, own, other, keep, got)


def slot_tables(route_ids, route_weight, side_index, per_side, experts):
    tokens, top = route_ids.shape
    entries = tokens * top
    ids = route_ids.reshape(-1)
    token = lax.broadcasted_iota(jnp.int32, (tokens, top), 0).reshape(-1)
    same = (ids[:, None] == ids[None, :]) & (token[:, None] > token[None, :])
    position = jnp.sum(same.astype(jnp.int32), axis=1)
    local = ids - side_index * per_side
    on_side = (local >= 0) & (local < per_side)
    dev = local // experts
    place = jnp.where(side_index == 0, dev, per_side // experts - 1 - dev)
    slot = jnp.where(on_side, (place * experts + local % experts) * CAP + position, -1)
    weights = jnp.where(on_side, route_weight.reshape(-1), 0.0)
    hit = slot[None, :] == lax.broadcasted_iota(jnp.int32, (per_side * CAP, entries), 0)
    source = tokens - jnp.sum(jnp.where(hit, tokens - token[None, :], 0), axis=1)
    return source, jnp.maximum(slot, 0), weights


def exchange(rows, dev_count):
    ahead = list(range(dev_count))
    groups = [ahead, [dev_count + d for d in reversed(ahead)]]
    return lax.all_to_all(
        rows,
        ("side", "dev"),
        split_axis=0,
        concat_axis=0,
        axis_index_groups=groups,
        tiled=True,
    )


def body(
    query,
    key_in,
    value,
    out_gate,
    decay_arg,
    beta_arg,
    decay_log,
    step_bias,
    states,
    norm_gain,
    out_weight,
    residual,
    post_gain,
    route_ids,
    route_weight,
    w_gate,
    w_up,
    w_down,
):
    tokens, width = residual.shape
    blocks = width // LANES
    dev_count = lax.axis_size("dev")
    experts = w_gate.shape[0]
    side_index = lax.axis_index("side")
    side = side_index.reshape(1)
    swap = [(0, 1), (1, 0)]
    own = delta_call(
        side,
        query,
        key_in,
        value,
        out_gate,
        decay_arg.T,
        beta_arg.T,
        decay_log.reshape(1, -1),
        step_bias.reshape(1, -1),
        states,
        norm_gain.reshape(1, -1),
        residual,
        out_weight,
    )
    other = lax.ppermute(own, "side", swap)
    source, slots, weights = slot_tables(
        route_ids, route_weight, side_index, dev_count * experts, experts
    )
    send_rows = pack_call(source, own, other, post_gain.reshape(blocks, LANES))
    received = exchange(send_rows, dev_count)
    expert_out = expert_call(
        received.reshape(dev_count, -1, LANES), w_gate, w_up, w_down
    ).reshape(received.shape)
    back = exchange(expert_out, dev_count)
    keep, send = gather_call(side, slots, weights, back, tokens, blocks)
    got = lax.ppermute(send, "side", swap)
    return last_call(side, own, other, keep, got, tokens)


def solution(mesh):
    in_specs = (
        P("dev", "side", None),
        P("dev", "side", None),
        P("dev", "side", None),
        P("dev", "side", None),
        P("dev", "side"),
        P("dev", "side"),
        P("side"),
        P("side"),
        P("dev", "side", None, None),
        P(),
        P("side", None),
        P("dev", None),
        P(),
        P("dev", None),
        P("dev", None),
        P(("side", "dev"), None, None),
        P(("side", "dev"), None, None),
        P(("side", "dev"), None, None),
    )
    out_specs = P("dev", "side")
    return jax.shard_map(body, mesh=mesh, in_specs=in_specs, out_specs=out_specs, check_vma=False)
```

```python
import jax
import jax.numpy as jnp
from jax import lax
from jax.experimental import pallas as pl
from jax.experimental.pallas import tpu as pltpu
from jax.sharding import PartitionSpec as P

CAP = 3
EPSILON = 1e-06
LANES = 128
TILE = 16
STEP_TOKENS = 2
MIB = 1 << 20


def in_hbm(*arrays):
    return [pltpu.with_memory_space_constraint(a, pltpu.HBM) for a in arrays]


def softplus(x):
    return jnp.maximum(x, 0.0) + jnp.log1p(jnp.exp(-jnp.abs(x)))


def sigmoid(x):
    return 1.0 / (1.0 + jnp.exp(-x))


def unit_rows(source):
    return source * lax.rsqrt(jnp.sum(source * source, -1, keepdims=True) + EPSILON)


def row_to_column(row):
    n = row.shape[1]
    square = jnp.broadcast_to(row, (n, n))
    on_diagonal = lax.broadcasted_iota(jnp.int32, (n, n), 0) == lax.broadcasted_iota(
        jnp.int32, (n, n), 1
    )
    return jnp.sum(jnp.where(on_diagonal, square, 0.0), axis=1, keepdims=True)


def delta_kernel(side_ref, *refs):
    small_hbm, state_hbm, weight_hbm, out_ref = refs[:10], refs[10], refs[11], refs[12]
    small_refs, refs = refs[13:23], refs[23:]
    state_ref, weight_ref, qstate_ref, kstate_ref, heads_ref, small_sem, state_sem, weight_sem = refs
    query_ref, key_ref, value_ref, gate_ref, decay_ref = small_refs[:5]
    beta_ref, log_ref, bias_ref, gain_ref, residual_ref = small_refs[5:]
    tokens, width = residual_ref.shape
    heads = value_ref.shape[1]
    key_heads = query_ref.shape[1]
    repeats = heads // key_heads
    size = query_ref.shape[2]
    parts = tokens // STEP_TOKENS
    smalls = [
        pltpu.make_async_copy(source, target, small_sem.at[i])
        for i, (source, target) in enumerate(zip(small_hbm, small_refs))
    ]
    loads = [
        pltpu.make_async_copy(
            state_hbm.at[pl.ds(i * STEP_TOKENS, STEP_TOKENS)],
            state_ref.at[pl.ds(i * STEP_TOKENS, STEP_TOKENS)],
            state_sem.at[i],
        )
        for i in range(parts)
    ]
    weight_load = pltpu.make_async_copy(weight_hbm, weight_ref, weight_sem)
    for load in smalls[:2] + loads[:2] + smalls[2:] + loads[2:] + [weight_load]:
        load.start()
    for load in smalls[:2]:
        load.wait()

    def rows(ref):
        return jnp.concatenate([ref[t].astype(jnp.float32) for t in range(tokens)], 0)

    query_unit = unit_rows(rows(query_ref)) * size ** (-0.5)
    key_unit = unit_rows(rows(key_ref))
    count = tokens * key_heads
    columns = jnp.concatenate([query_unit, key_unit], 0).T
    products = jnp.broadcast_to(
        jnp.sum(query_unit * key_unit, -1, keepdims=True), (count, size)
    )
    for r in range(repeats):
        heads_ref[pl.ds(r, count, stride=repeats), :] = products
    for i in range(parts):
        loads[i].wait()
        for t in range(i * STEP_TOKENS, (i + 1) * STEP_TOKENS):
            for k in range(key_heads):
                at = t * key_heads + k
                qcol = jnp.broadcast_to(columns[:, at : at + 1], (size, size))
                at = at + count
                kcol = jnp.broadcast_to(columns[:, at : at + 1], (size, size))
                for r in range(repeats):
                    h = k * repeats + r
                    state = state_ref[t, h]
                    at = t * heads + h
                    qstate_ref[at : at + 1, :] = jnp.sum(qcol * state, axis=0, keepdims=True)
                    kstate_ref[at : at + 1, :] = jnp.sum(kcol * state, axis=0, keepdims=True)

    for load in smalls[2:]:
        load.wait()
    retain_all = jnp.exp(
        -jnp.exp(row_to_column(log_ref[...]))
        * softplus(decay_ref[...] + row_to_column(bias_ref[...]))
    )
    rate_all = sigmoid(beta_ref[...])

    def per_head(table):
        return jnp.concatenate(
            [jnp.broadcast_to(table[:, t : t + 1], (heads, size)) for t in range(tokens)], 0
        )

    retain, rate = per_head(retain_all), per_head(rate_all)
    correct = rate * (rows(value_ref) - retain * kstate_ref[...])
    attend = retain * qstate_ref[...] + heads_ref[...] * correct
    inv_rms = lax.rsqrt(jnp.mean(attend * attend, -1, keepdims=True) + EPSILON)
    gate = rows(gate_ref)
    heads_ref[...] = attend * inv_rms * gain_ref[...] * (gate * sigmoid(gate))
    gated_out = jnp.concatenate(
        [heads_ref[pl.ds(h, tokens, stride=heads), :] for h in range(heads)], 1
    ).astype(jnp.bfloat16)
    weight_load.wait()
    side = side_ref[0]
    blocks = width // LANES
    wide = 4 * LANES
    for n in range(width // wide):
        part = jnp.dot(
            gated_out,
            weight_ref[:, n * wide : (n + 1) * wide],
            preferred_element_type=jnp.float32,
        )
        kept = residual_ref[:, n * wide : (n + 1) * wide].astype(jnp.float32)
        part = part + jnp.where(side == 0, kept, 0.0)
        for f in range(4):
            out_ref[pl.ds(n * 4 + f, tokens, stride=blocks), :] = part[
                :, f * LANES : (f + 1) * LANES
            ]


def delta_call(side, query, key_in, value, gate, decay, beta, log, bias, states, gain, residual, weight):
    tokens, heads, size = value.shape
    width = residual.shape[1]
    small = (query, key_in, value, gate, decay, beta, log, bias, gain, residual)
    vmem = pl.BlockSpec(memory_space=pltpu.VMEM)
    pairs = pltpu.VMEM((tokens * heads, size), jnp.float32)
    return pl.pallas_call(
        delta_kernel,
        out_shape=jax.ShapeDtypeStruct((tokens * width // LANES, LANES), jnp.float32),
        in_specs=[pl.BlockSpec(memory_space=pltpu.SMEM)]
        + [pl.BlockSpec(memory_space=pl.ANY)] * (len(small) + 2),
        out_specs=vmem,
        scratch_shapes=[pltpu.VMEM(a.shape, a.dtype) for a in small]
        + [
            pltpu.VMEM(states.shape, states.dtype),
            pltpu.VMEM(weight.shape, weight.dtype),
            pairs,
            pairs,
            pairs,
            pltpu.SemaphoreType.DMA((len(small),)),
            pltpu.SemaphoreType.DMA((tokens // STEP_TOKENS,)),
            pltpu.SemaphoreType.DMA,
        ],
        compiler_params=pltpu.CompilerParams(vmem_limit_bytes=24 * MIB),
        name="delta",
    )(side, *in_hbm(*small, states, weight))


def pack_kernel(source_ref, own_ref, other_ref, gain_ref, out_ref, tiles_ref):
    blocks = gain_ref.shape[0]
    tokens = own_ref.shape[0] // blocks
    for t in range(tokens):
        rows = slice(t * blocks, (t + 1) * blocks)
        hidden = own_ref[rows, :] + other_ref[rows, :]
        mean = jnp.sum(
            jnp.sum(hidden * hidden, axis=0, keepdims=True), axis=1, keepdims=True
        ) * (1.0 / (blocks * LANES))
        tiles_ref[rows, :] = (hidden * lax.rsqrt(mean + EPSILON) * gain_ref[...]).astype(
            jnp.bfloat16
        )
    tiles_ref[tokens * blocks :, :] = jnp.zeros((blocks, LANES), jnp.bfloat16)
    slots = out_ref.shape[0] // blocks
    for s in range(slots):
        at = pl.multiple_of(source_ref[s] * blocks, blocks)
        out_ref[s * blocks : (s + 1) * blocks, :] = tiles_ref[pl.ds(at, blocks), :]


def pack_call(source, own, other, gain):
    blocks = gain.shape[0]
    slots = source.shape[0]
    vmem = pl.BlockSpec(memory_space=pltpu.VMEM)
    return pl.pallas_call(
        pack_kernel,
        out_shape=jax.ShapeDtypeStruct((slots * blocks, LANES), jnp.bfloat16),
        in_specs=[pl.BlockSpec(memory_space=pltpu.SMEM), vmem, vmem, vmem],
        out_specs=vmem,
        scratch_shapes=[pltpu.VMEM((own.shape[0] + blocks, LANES), jnp.bfloat16)],
        compiler_params=pltpu.CompilerParams(vmem_limit_bytes=16 * MIB),
        name="pack",
    )(source, own, other, gain)


def expert_kernel(x_ref, gate_ref, up_hbm, down_hbm, out_ref, up_ref, down_ref, rows_ref, sems):
    experts, width, units = gate_ref.shape
    sources = x_ref.shape[0]
    blocks = width // LANES
    groups = sources // TILE
    count = groups * CAP * TILE
    wide = 4 * LANES
    copies = []
    for e in range(experts):
        copies.append(pltpu.make_async_copy(up_hbm.at[e], up_ref.at[e], sems.at[2 * e]))
        copies.append(pltpu.make_async_copy(down_hbm.at[e], down_ref.at[e], sems.at[2 * e + 1]))
    for copy in copies[:2]:
        copy.start()
    row = lax.broadcasted_iota(jnp.int32, (TILE * blocks, TILE * blocks), 0)
    column = lax.broadcasted_iota(jnp.int32, (TILE * blocks, TILE * blocks), 1)
    swap = jnp.where((row % TILE) * TILE + row // TILE == column, 1.0, 0.0).astype(jnp.bfloat16)
    places = [(g, c) for g in range(groups) for c in range(CAP)]

    def turn(pair):
        turned = jnp.dot(swap, jnp.concatenate(pair, 1), preferred_element_type=jnp.float32)
        turned = turned.astype(jnp.bfloat16)
        return turned[:, :LANES], turned[:, LANES:]

    def place_of(e, g, c):
        return g * TILE, (e * CAP + c) * blocks

    for e in range(experts):
        for n in range(0, len(places), 2):
            pair = []
            for g, c in places[n : n + 2]:
                top, at = place_of(e, g, c)
                block = x_ref[top : top + TILE, at : at + blocks, :]
                pair.append(block.reshape(TILE * blocks, LANES))
            for i, turned in enumerate(turn(pair)):
                r = e * count + (n + i) * TILE
                for f in range(blocks):
                    rows_ref[r : r + TILE, f * LANES : (f + 1) * LANES] = turned[
                        f * TILE : (f + 1) * TILE
                    ]
        x = rows_ref[e * count : (e + 1) * count, :]
        gate = jnp.dot(x, gate_ref[e], preferred_element_type=jnp.float32)
        copies[2 * e].wait()
        if e + 1 < experts:
            copies[2 * e + 2].start()
        up = jnp.dot(x, up_ref[e], preferred_element_type=jnp.float32)
        inner = (gate * sigmoid(gate) * up).astype(jnp.bfloat16)
        copies[2 * e + 1].wait()
        if e + 1 < experts:
            copies[2 * e + 3].start()
        for n in range(width // wide):
            y = jnp.dot(
                inner, down_ref[e, :, n * wide : (n + 1) * wide], preferred_element_type=jnp.float32
            )
            rows_ref[e * count : (e + 1) * count, n * wide : (n + 1) * wide] = y.astype(
                jnp.bfloat16
            )
        for n in range(0, len(places), 2):
            pair = []
            for i in range(2):
                r = e * count + (n + i) * TILE
                pair.append(
                    jnp.concatenate(
                        [
                            rows_ref[r : r + TILE, f * LANES : (f + 1) * LANES]
                            for f in range(blocks)
                        ],
                        0,
                    )
                )
            for (g, c), turned in zip(places[n : n + 2], turn(pair)):
                top, at = place_of(e, g, c)
                out_ref[top : top + TILE, at : at + blocks, :] = turned.reshape(
                    TILE, blocks, LANES
                )


def expert_call(received, w_gate, w_up, w_down):
    experts, width, units = w_gate.shape
    vmem = pl.BlockSpec(memory_space=pltpu.VMEM)
    hbm = pl.BlockSpec(memory_space=pl.ANY)
    slots = received.shape[0] * CAP * experts
    return pl.pallas_call(
        expert_kernel,
        out_shape=jax.ShapeDtypeStruct(received.shape, received.dtype),
        in_specs=[vmem, vmem, hbm, hbm],
        out_specs=vmem,
        scratch_shapes=[
            pltpu.VMEM(w_up.shape, w_up.dtype),
            pltpu.VMEM(w_down.shape, w_down.dtype),
            pltpu.VMEM((slots, width), jnp.bfloat16),
            pltpu.SemaphoreType.DMA((2 * experts,)),
        ],
        compiler_params=pltpu.CompilerParams(vmem_limit_bytes=24 * MIB),
        name="experts",
    )(received, w_gate, *in_hbm(w_up, w_down))


def half_sums(take_high, slot_ref, weight_ref, back_ref, tokens, blocks, store):
    half = blocks // 2
    top = slot_ref.shape[0] // tokens
    for t in range(tokens):
        total = jnp.zeros((half, LANES), jnp.float32)
        for k in range(top):
            at = pl.multiple_of(slot_ref[t * top + k] * blocks, blocks)
            tile = back_ref[pl.ds(at, blocks), :].astype(jnp.float32)
            tile = jnp.where(take_high, tile[half:], tile[:half])
            total = total + weight_ref[t * top + k] * tile
        store(t, total)


def send_kernel(side_ref, slot_ref, weight_ref, back_ref, out_ref, *, blocks):
    half = blocks // 2

    def store(t, total):
        out_ref[t * half : (t + 1) * half, :] = total

    tokens = out_ref.shape[0] // half
    half_sums(side_ref[0] == 0, slot_ref, weight_ref, back_ref, tokens, blocks, store)


def keep_kernel(side_ref, slot_ref, weight_ref, back_ref, own_ref, other_ref, out_ref, *, blocks):
    half = blocks // 2
    side = side_ref[0]

    def store(t, total):
        at = pl.multiple_of((2 * t + side) * half, half)
        hidden = own_ref[pl.ds(at, half), :] + other_ref[pl.ds(at, half), :]
        out_ref[t * half : (t + 1) * half, :] = hidden + total

    tokens = out_ref.shape[0] // half
    half_sums(side == 1, slot_ref, weight_ref, back_ref, tokens, blocks, store)


def half_call(kernel, name, side, slots, weights, back, *hidden, tokens, blocks):
    vmem = pl.BlockSpec(memory_space=pltpu.VMEM)
    smem = pl.BlockSpec(memory_space=pltpu.SMEM)
    entries = slots.shape[0]
    return pl.pallas_call(
        lambda *refs: kernel(*refs, blocks=blocks),
        out_shape=jax.ShapeDtypeStruct((tokens * blocks // 2, LANES), jnp.float32),
        in_specs=[smem, smem, smem, vmem] + [vmem] * len(hidden),
        out_specs=vmem,
        compiler_params=pltpu.CompilerParams(vmem_limit_bytes=16 * MIB),
        cost_estimate=pl.CostEstimate(
            flops=2 * entries * blocks * LANES,
            bytes_accessed=2 * entries * blocks * LANES,
            transcendentals=0,
        ),
        name=name,
    )(side, slots, weights, back, *hidden)


def last_kernel(keep_ref, got_ref, out_ref, sums_ref):
    tokens, width = out_ref.shape
    half = width // LANES
    sums_ref[...] = keep_ref[...] + got_ref[...]
    for f in range(half):
        out_ref[:, f * LANES : (f + 1) * LANES] = sums_ref[
            pl.ds(f, tokens, stride=half), :
        ].astype(jnp.bfloat16)


def last_call(keep, got, tokens):
    vmem = pl.BlockSpec(memory_space=pltpu.VMEM)
    return pl.pallas_call(
        last_kernel,
        out_shape=jax.ShapeDtypeStruct((tokens, keep.size // tokens), jnp.bfloat16),
        in_specs=[vmem, vmem],
        out_specs=vmem,
        scratch_shapes=[pltpu.VMEM(keep.shape, jnp.float32)],
        compiler_params=pltpu.CompilerParams(vmem_limit_bytes=16 * MIB),
        name="last",
    )(keep, got)


def slot_tables(route_ids, route_weight, side_index, per_side, experts):
    tokens, top = route_ids.shape
    entries = tokens * top
    ids = route_ids.reshape(-1)
    token = lax.broadcasted_iota(jnp.int32, (tokens, top), 0).reshape(-1)
    same = (ids[:, None] == ids[None, :]) & (token[:, None] > token[None, :])
    position = jnp.sum(same.astype(jnp.int32), axis=1)
    local = ids - side_index * per_side
    on_side = (local >= 0) & (local < per_side)
    dev = local // experts
    place = jnp.where(side_index == 0, dev, per_side // experts - 1 - dev)
    slot = jnp.where(on_side, (place * experts + local % experts) * CAP + position, -1)
    weights = jnp.where(on_side, route_weight.reshape(-1), 0.0)
    hit = slot[None, :] == lax.broadcasted_iota(jnp.int32, (per_side * CAP, entries), 0)
    source = tokens - jnp.sum(jnp.where(hit, tokens - token[None, :], 0), axis=1)
    return source, jnp.maximum(slot, 0), weights


def exchange(rows, dev_count):
    ahead = list(range(dev_count))
    groups = [ahead, [dev_count + d for d in reversed(ahead)]]
    return lax.all_to_all(
        rows,
        ("side", "dev"),
        split_axis=0,
        concat_axis=0,
        axis_index_groups=groups,
        tiled=True,
    )


def body(
    query,
    key_in,
    value,
    out_gate,
    decay_arg,
    beta_arg,
    decay_log,
    step_bias,
    states,
    norm_gain,
    out_weight,
    residual,
    post_gain,
    route_ids,
    route_weight,
    w_gate,
    w_up,
    w_down,
):
    tokens, width = residual.shape
    blocks = width // LANES
    dev_count = lax.axis_size("dev")
    experts = w_gate.shape[0]
    side_index = lax.axis_index("side")
    side = side_index.reshape(1)
    swap = [(0, 1), (1, 0)]
    own = delta_call(
        side,
        query,
        key_in,
        value,
        out_gate,
        decay_arg.T,
        beta_arg.T,
        decay_log.reshape(1, -1),
        step_bias.reshape(1, -1),
        states,
        norm_gain.reshape(1, -1),
        residual,
        out_weight,
    )
    other = lax.ppermute(own, "side", swap)
    source, slots, weights = slot_tables(
        route_ids, route_weight, side_index, dev_count * experts, experts
    )
    send_rows = pack_call(source, own, other, post_gain.reshape(blocks, LANES))
    received = exchange(send_rows, dev_count)
    expert_out = expert_call(
        received.reshape(dev_count, -1, LANES), w_gate, w_up, w_down
    ).reshape(received.shape)
    back = exchange(expert_out, dev_count)
    sizes = dict(tokens=tokens, blocks=blocks)
    send = half_call(send_kernel, "send", side, slots, weights, back, **sizes)
    got = lax.ppermute(send, "side", swap)
    keep = half_call(keep_kernel, "keep", side, slots, weights, back, own, other, **sizes)
    return last_call(keep, got, tokens)


def solution(mesh):
    in_specs = (
        P("dev", "side", None),
        P("dev", "side", None),
        P("dev", "side", None),
        P("dev", "side", None),
        P("dev", "side"),
        P("dev", "side"),
        P("side"),
        P("side"),
        P("dev", "side", None, None),
        P(),
        P("side", None),
        P("dev", None),
        P(),
        P("dev", None),
        P("dev", None),
        P(("side", "dev"), None, None),
        P(("side", "dev"), None, None),
        P(("side", "dev"), None, None),
    )
    out_specs = P("dev", "side")
    return jax.shard_map(body, mesh=mesh, in_specs=in_specs, out_specs=out_specs, check_vma=False)
```
